256 devices in a mesh: grp: 32 (over y_lo, z, core), blk: 8 (over y_hi, x).
Axes of the slice: x: 4, y: 4 (y_hi: 2, y_lo: 2; y = y_hi * 2 + y_lo), z: 8, core: 2. Of those that a mesh axis runs over, the one named last changes fastest.
Arguments:
- tiles: bfloat16 [16384, 16384], P(('blk', 'grp'))
- exponents: int32 [256, 256], P(('blk', 'grp')), may hold values from -2 to 2, as said below
- rhs: bfloat16 [32, 16384], P(None, ('blk', 'grp'))
- elem_frac: int32 [16384], P(('blk', 'grp')), may hold values from 0 to 63
- compliance: float32 [64], replicated, may hold values from 0.3 to 1.5
- scen_map: int32 [32], replicated, may hold values from 0 to 31, each once
Outputs:
- basis: bfloat16 [32, 16384], P(None, ('blk', 'grp'))
- root_mean: float32 [12, 32], replicated
The draws below stay inside these ranges and needn't reach their ends.
Inputs may be any that keep to these rules, and one draw needn't show every extreme that they name: Integer tile exponents. `scen_map`: each scenario row taken once.
All inputs are finite; a program needn't handle non-finite values.
Results may differ from the reference program's by a relative error of at most 0.014.
Values may be sent and summed in bfloat16 or wider, within the bound.
A program may use at most 64 MiB of HBM per device.

```python
import math
import jax
import jax.numpy as jnp
from jax import lax

S = 32
FRACS = 64
STEPS = 12
TILE = 64
ELEMS = 16384


def tile_exponents(key):
    return jax.random.randint(key, (ELEMS // TILE, ELEMS // TILE), -2, 3).astype(jnp.int32)


def draw_exponents(key, part):
    return tile_exponents(key)


def draw_tiles(key, part):
    expo = tile_exponents(key)
    key = jax.random.fold_in(key, 11)
    key_off, key_diag = jax.random.split(key)
    off_part = jax.random.normal(key_off, (ELEMS, ELEMS), jnp.float32) * (0.45 / ELEMS ** 0.5)
    diag_part = jax.random.uniform(key_diag, (ELEMS,), jnp.float32, 1.5, 2.5)
    index = jnp.arange(ELEMS)
    full = off_part.at[index, index].add(diag_part)
    tile_count = ELEMS // TILE
    inverse = jnp.exp2(-expo.astype(jnp.float32))
    full = full.reshape(tile_count, TILE, tile_count, TILE) * inverse[:, None, :, None]
    return full.reshape(ELEMS, ELEMS).astype(jnp.bfloat16)


def draw_rhs(key, part):
    key = jax.random.fold_in(key, 5)
    key_a = jax.random.fold_in(key, 0)
    row_scale = 0.5 + 1.5 * jnp.arange(ELEMS, dtype=jnp.float32) / ELEMS
    values = jax.random.normal(key_a, (S, ELEMS), jnp.float32)
    return jnp.clip(values * row_scale[None, :], -8.0, 8.0).astype(jnp.bfloat16)


def plant(drawn, rng, low, high):
    shape = drawn.shape
    index_at = [jax.random.randint(jax.random.fold_in(rng, axis), (), 0, shape[axis]) for axis in range(len(shape))]
    drawn = drawn.at[tuple(index_at)].set(low)
    longest = shape.index(max(shape))
    index_at[longest] = (index_at[longest] + 1) % shape[longest]
    return drawn.at[tuple(index_at)].set(high)


def setup_inputs(seed: int = 0) -> dict:
    key_list = jax.random.split(jax.random.key(seed), 7)
    return {
        "tiles": draw_tiles(jax.random.fold_in(key_list[6], 71), 0),
        "exponents": draw_exponents(jax.random.fold_in(key_list[6], 71), 0),
        "rhs": draw_rhs(jax.random.fold_in(key_list[6], 71), 0),
        "elem_frac": plant(jax.random.randint(key_list[3], (ELEMS,), 0, FRACS), jax.random.fold_in(key_list[3], 1), 0, FRACS - 1).astype(jnp.int32),
        "compliance": jnp.clip(jnp.exp(jax.random.uniform(key_list[4], (FRACS,), jnp.float32, math.log(0.3), math.log(1.5))), 0.3, 1.5),
        "scen_map": jax.random.permutation(key_list[5], S).astype(jnp.int32),
    }


def reference(tiles, exponents, rhs, elem_frac, compliance, scen_map):
    tile_count = ELEMS // TILE
    tile_scale = jnp.exp2(exponents.astype(jnp.float32))
    scen_pick = (scen_map[None, :] == jnp.arange(S, dtype=jnp.int32)[:, None]).astype(jnp.float32)
    basis = jnp.dot(scen_pick.T, rhs.astype(jnp.float32), precision=lax.Precision.HIGHEST).astype(jnp.bfloat16)
    diag_term = compliance[elem_frac]
    tile_rows = tiles.reshape(tile_count, TILE, ELEMS)

    def one_band(band):
        mantissa, gains = band
        scaled = (mantissa.astype(jnp.float32).reshape(TILE, tile_count, TILE) * gains[None, :, None]).reshape(TILE, ELEMS)
        return scaled
    history = []
    for iteration in range(STEPS):
        vector = basis.astype(jnp.float32)

        def band_product(band):
            scaled = one_band(band)
            return lax.dot_general(vector, scaled, (((1,), (1,)), ((), ())), precision=lax.Precision.HIGHEST)
        bands = lax.map(band_product, (tile_rows, tile_scale))
        image = jnp.transpose(bands, (1, 0, 2)).reshape(S, ELEMS) + diag_term[None, :] * vector
        root_mean = jnp.sqrt(lax.optimization_barrier(jnp.sum(image * image, axis=1)) / ELEMS + 1e-06)
        history.append(root_mean)
        basis = (image / root_mean[:, None]).astype(jnp.bfloat16)
    return (basis, jnp.stack(history))
```

```python
import functools

import jax
import jax.numpy as jnp
from jax import lax
from jax.experimental import pallas as pl
from jax.experimental.pallas import tpu as pltpu
from jax.sharding import PartitionSpec as P

STEPS = 12
NX, NY, NZ = 4, 4, 8
CHIPS = NX * NY * NZ
HALF = 16
ROWS = 128
KEEP = 64
ALL = CHIPS * ROWS
MESH = pl.DeviceIdType.MESH
F32, BF16 = jnp.float32, jnp.bfloat16


def hops(delta):
    return sum(min(d, n - d) for d, n in zip(delta, (NX, NY, NZ)))


DELTAS = sorted(
    [(dx, dy, dz) for dz in range(NZ) for dx in range(NX) for dy in range(NY) if dx or dy or dz],
    key=lambda d: -hops(d),
)


def device(x, y, z, core):
    return {"blk": lax.div(y, 2) * NX + x, "grp": lax.rem(y, 2) * 16 + z * 2 + core}


def iota(shape, dim):
    return lax.broadcasted_iota(jnp.int32, shape, dim)


def as_column(row):
    n = row.shape[1]
    eye = iota((n, n), 0) == iota((n, n), 1)
    return jnp.sum(jnp.where(eye, jnp.broadcast_to(row, (n, n)), 0.0), axis=1, keepdims=True)


def kernel(
    tiles, expo, rhs, frac, comp, smap, basis_out, rms_out,
    amat, vbuf, start, started, diag_mine, diag_other, gains, norms, history, last,
    load_sem, swap_send, swap_recv, send, recv,
):
    blk, grp = lax.axis_index("blk"), lax.axis_index("grp")
    x, y = lax.rem(blk, NX), lax.div(blk, NX) * 2 + lax.div(grp, 16)
    z, core = lax.rem(lax.div(grp, 2), NZ), lax.rem(grp, 2)
    other = 1 - core
    mine = lax.div(y, 2) * 64 + x * 16 + lax.rem(y, 2) * 8 + z
    sibling = device(x, y, z, other)
    peers = [
        device(lax.rem(x + dx, NX), lax.rem(y + dy, NY), lax.rem(z + dz, NZ), core)
        for dx, dy, dz in DELTAS
    ]

    own_rows = pl.ds(pl.multiple_of(core * KEEP, KEEP), KEEP)
    load = pltpu.make_async_copy(tiles, amat.at[own_rows], load_sem)
    load.start()

    barrier = pltpu.get_barrier_semaphore()
    for peer in [sibling, *peers]:
        pl.semaphore_signal(barrier, inc=1, device_id=peer, device_id_type=MESH)

    picked = as_column(smap[...].astype(F32)) == iota((32, 32), 1).astype(F32)
    first = jnp.dot(
        jnp.where(picked, 1.0, 0.0).astype(BF16), rhs[...], preferred_element_type=F32
    )
    first = jnp.concatenate([first, first], axis=1).astype(BF16)
    start[0] = first[:HALF]
    start[1] = first[HALF:]
    member = iota((64, KEEP), 0) == frac[...]
    local_diag = jnp.sum(
        jnp.where(member, as_column(comp[...]), 0.0), axis=0, keepdims=True
    )
    diag_mine[...] = jnp.broadcast_to(
        jnp.concatenate([local_diag, local_diag], axis=1), (8, ROWS)
    )
    scale_row = jnp.exp2(expo[...].astype(F32)).astype(BF16).astype(F32)
    spread = jnp.where(
        (iota((CHIPS, 256), 1) >> 1) == iota((CHIPS, 256), 0), scale_row, 0.0
    ).astype(BF16)
    sides = jnp.where(
        (iota((256, ROWS), 0) & 1) == (iota((256, ROWS), 1) >> 6), 1.0, 0.0
    ).astype(BF16)
    gains[...] = jnp.dot(spread, sides, preferred_element_type=F32)

    pl.semaphore_wait(barrier, 1 + len(peers))

    def swap(src, dst, i):
        return pltpu.make_async_remote_copy(
            src, dst, swap_send.at[i], swap_recv.at[i], device_id=sibling, device_id_type=MESH
        )

    swap_start = swap(start.at[other], started, 0)
    swap_start.start()
    swap_diag = swap(diag_mine, diag_other, 1)
    swap_diag.start()

    ours = (iota((1, ROWS), 1) >> 6) == core

    def whole(sem, par):
        part = vbuf.at[par, pl.ds(0, CHIPS - 1)]
        return pltpu.make_async_copy(part, part, sem.at[par])

    def post(par):
        block = vbuf.at[par, mine]
        for peer in peers:
            pltpu.make_async_remote_copy(
                block, block, send.at[par], recv.at[par], device_id=peer, device_id_type=MESH
            ).start()

    swap_start.wait()
    vbuf[0, mine] = jnp.where(ours, start[core], started[...])
    post(0)

    load.wait()

    def scale(b, _):
        gain = jnp.broadcast_to(gains[pl.ds(b, 1), :], (16, ROWS)).astype(BF16)
        columns = pl.ds(pl.multiple_of(b * ROWS, ROWS), ROWS)
        for i in range(KEEP // 16):
            rows = pl.ds(pl.multiple_of(core * KEEP + 16 * i, 16), 16)
            amat[rows, columns] = amat[rows, columns] * gain
        return 0

    lax.fori_loop(0, CHIPS, scale, 0, unroll=4)
    swap_rows = swap(amat.at[own_rows], amat.at[own_rows], 2)
    swap_rows.start()
    swap_diag.wait()
    diag = jnp.where(ours, diag_mine[0:1], diag_other[0:1])
    swap_rows.wait()

    lane = iota((HALF, ROWS), 1)

    def product(step, par):
        whole(recv, par).wait()
        sums = [jnp.zeros((HALF, ROWS), F32) for _ in range(4)]
        for b in range(CHIPS):
            value = vbuf[par, b].astype(F32)
            sums[b % 4] += value * value
        squares = jnp.sum((sums[0] + sums[1]) + (sums[2] + sums[3]), axis=1, keepdims=True)
        root = jnp.sqrt(squares / ALL + 1e-06)
        opening = step == 0
        history[core] = jnp.where(lane == step - 1, root, history[core])
        root = jnp.where(opening, 1.0, root)
        shrink = jnp.exp2(-jnp.floor(jnp.log2(root))).astype(BF16).astype(F32)
        inverse = 1.0 / root
        spread16 = jnp.broadcast_to(shrink, (HALF, ROWS)).astype(BF16)
        total = jnp.zeros((HALF, ROWS), F32)
        group = 16
        for g in range(CHIPS // group):
            part = jnp.concatenate(
                [vbuf[par, g * group + i] * spread16 for i in range(group)], axis=1
            )
            total += lax.dot_general(
                part, amat[:, g * group * ROWS : (g + 1) * group * ROWS],
                (((1,), (1,)), ((), ())), preferred_element_type=F32,
            )
        own = vbuf[par, mine].astype(F32)
        return total * (inverse / shrink) + diag * (own * inverse)

    history[core] = jnp.zeros((HALF, ROWS), F32)

    def advance(step, _):
        par = lax.rem(step, 2)
        image = product(step, par)

        @pl.when(step >= 1)
        def _():
            whole(send, 1 - par).wait()

        vbuf[1 - par, mine] = image.astype(BF16)
        post(1 - par)
        return 0

    lax.fori_loop(0, STEPS - 1, advance, 0)
    image = product(STEPS - 1, (STEPS - 1) % 2)

    eye = iota((HALF, ROWS), 0) == lane
    square = jnp.sum(image * image, axis=1, keepdims=True)
    norms[pl.ds(mine, 1), :] = jnp.sum(jnp.where(eye, square, 0.0), axis=0, keepdims=True)
    whole(send, 0).wait()
    row = norms.at[pl.ds(mine, 1)]
    for peer in peers:
        pltpu.make_async_remote_copy(
            row, row, send.at[0], recv.at[0], device_id=peer, device_id_type=MESH
        ).start()
    rows = norms.at[pl.ds(0, CHIPS - 1)]
    pltpu.make_async_copy(rows, rows, recv.at[0]).wait()
    total = jnp.sum(norms[...], axis=0, keepdims=True)
    squares = jnp.sum(jnp.where(eye, total, 0.0), axis=1, keepdims=True)
    root = jnp.sqrt(squares / ALL + 1e-06)
    history[core] = jnp.where(lane == STEPS - 1, root, history[core])
    last[core] = (image / root).astype(BF16)
    swap_last = swap(last.at[core], last.at[core], 3)
    swap_history = swap(history.at[core], history.at[core], 4)
    swap_last.start()
    swap_history.start()
    pltpu.make_async_copy(rows, rows, send.at[0]).wait()
    whole(send, 1).wait()
    swap_last.wait()
    swap_history.wait()
    result = jnp.concatenate([last[0], last[1]], axis=0).astype(F32)
    basis_out[...] = jnp.where(core == 0, result[:, :KEEP], result[:, KEEP:]).astype(BF16)
    table = jnp.concatenate([history[0], history[1]], axis=0)
    rms_out[...] = table.T[:STEPS]


def on_device(tiles, exponents, rhs, elem_frac, compliance, scen_map):
    vmem = pl.BlockSpec(memory_space=pltpu.VMEM)
    return tuple(
        pl.pallas_call(
            kernel,
            out_shape=(
                jax.ShapeDtypeStruct((32, KEEP), BF16),
                jax.ShapeDtypeStruct((STEPS, 32), F32),
            ),
            in_specs=[pl.BlockSpec(memory_space=pl.ANY)] + [vmem] * 5,
            out_specs=(vmem, vmem),
            scratch_shapes=[
                pltpu.VMEM((ROWS, ALL), BF16),
                pltpu.VMEM((2, CHIPS, HALF, ROWS), BF16),
                pltpu.VMEM((2, HALF, ROWS), BF16),
                pltpu.VMEM((HALF, ROWS), BF16),
                pltpu.VMEM((8, ROWS), F32),
                pltpu.VMEM((8, ROWS), F32),
                pltpu.VMEM((CHIPS, ROWS), F32),
                pltpu.VMEM((CHIPS, ROWS), F32),
                pltpu.VMEM((2, HALF, ROWS), F32),
                pltpu.VMEM((2, HALF, ROWS), BF16),
                pltpu.SemaphoreType.DMA,
                pltpu.SemaphoreType.DMA((5,)),
                pltpu.SemaphoreType.DMA((5,)),
                pltpu.SemaphoreType.DMA((2,)),
                pltpu.SemaphoreType.DMA((2,)),
            ],
            compiler_params=pltpu.CompilerParams(
                collective_id=0, has_side_effects=True, vmem_limit_bytes=32 << 20
            ),
            cost_estimate=pl.CostEstimate(
                flops=2 * STEPS * 32 * KEEP * ALL, bytes_accessed=2 * KEEP * ALL, transcendentals=0
            ),
            name="krylov",
        )(
            tiles,
            exponents,
            rhs,
            elem_frac.reshape(1, KEEP),
            compliance.reshape(1, 64),
            scen_map.reshape(1, 32),
        )
    )


def solution(mesh):
    placed = (
        P(("blk", "grp"), None),
        P(("blk", "grp"), None),
        P(None, ("blk", "grp")),
        P(("blk", "grp")),
        P(),
        P(),
    )
    return jax.shard_map(
        on_device,
        mesh=mesh,
        in_specs=placed,
        out_specs=(P(None, ("blk", "grp")), P()),
        check_vma=False,
    )
```

```python
import functools

import jax
import jax.numpy as jnp
from jax import lax
from jax.experimental import pallas as pl
from jax.experimental.pallas import tpu as pltpu
from jax.sharding import PartitionSpec as P

STEPS = 12
NX, NY, NZ = 4, 4, 8
CHIPS = NX * NY * NZ
HALF = 16
ROWS = 128
KEEP = 64
ALL = CHIPS * ROWS
MESH = pl.DeviceIdType.MESH
F32, BF16 = jnp.float32, jnp.bfloat16


def hops(delta):
    return sum(min(d, n - d) for d, n in zip(delta, (NX, NY, NZ)))


ORDER = (0, 1, 7, 2, 6, 3, 5, 4)
PLACE = {dz: i for i, dz in enumerate(ORDER)}
GROUPS = ((1, 3), (3, 7))
PLANE = sorted(
    [(dx, dy, 0) for dx in range(NX) for dy in range(NY) if dx or dy], key=lambda d: -hops(d)
)
LISTED = [p for lo, hi in GROUPS for p in range(lo, hi)]
ABOVE = [dz for dz in (3, 5, 2, 6, 1, 7, 4) if PLACE[(NZ - dz) % NZ] in LISTED]
DIRECT = sorted(
    [
        (dx, dy, dz)
        for dz in range(NZ)
        for dx in range(NX)
        for dy in range(NY)
        if (dx or dy or dz) and PLACE[(NZ - dz) % NZ] not in LISTED
    ],
    key=lambda d: -hops(d),
)
DUE = len(DIRECT) + len(PLANE) * len(LISTED)
SLOTS = 3


def device(blk, grp):
    return {"blk": blk, "grp": grp}


def iota(shape, dim):
    return lax.broadcasted_iota(jnp.int32, shape, dim)


def as_column(row):
    n = row.shape[1]
    eye = iota((n, n), 0) == iota((n, n), 1)
    return jnp.sum(jnp.where(eye, jnp.broadcast_to(row, (n, n)), 0.0), axis=1, keepdims=True)


def kernel(
    tiles, expo_in, rhs_in, frac_in, comp_in, smap_in, basis_out, rms_out,
    expo, rhs, frac, comp, smap, raw, amat, vbuf, start, started, diag_mine, diag_other, gains, norms, history, last,
    load_sem, swap_send, swap_recv, send, recv, relay, norm_sem,
):
    blk, grp = lax.axis_index("blk"), lax.axis_index("grp")
    x, y = lax.rem(blk, NX), lax.div(blk, NX) * 2 + lax.div(grp, 16)
    z, core = lax.rem(lax.div(grp, 2), NZ), lax.rem(grp, 2)
    other = 1 - core
    mine = lax.div(y, 2) * 64 + x * 16 + lax.rem(y, 2) * 8 + z
    sibling = device(blk, grp + 1 - 2 * core)
    xs = [lax.rem(x + d, NX) for d in range(NX)]
    ys = [lax.rem(y + d, NY) for d in range(NY)]
    blks = [[lax.div(ys[dy], 2) * NX + xs[dx] for dy in range(NY)] for dx in range(NX)]
    low = [lax.rem(y, 2) * 16 + core, (1 - lax.rem(y, 2)) * 16 + core]
    grps = [[low[d] + 2 * lax.rem(z + dz, NZ) for dz in range(NZ)] for d in range(2)]

    def peer(delta):
        dx, dy, dz = delta
        return device(blks[dx][dy], grps[dy % 2][dz])

    everyone = sorted((dx, dy, dz) for dz in range(NZ) for dx in range(NX) for dy in range(NY))[1:]
    everyone.sort(key=lambda d: -hops(d))
    base = mine - z

    own_rows = pl.ds(pl.multiple_of(core * KEEP, KEEP), KEEP)
    load = pltpu.make_async_copy(tiles, raw.at[own_rows], load_sem.at[0])
    load.start()
    small = [
        pltpu.make_async_copy(src, dst, load_sem.at[1 + i])
        for i, (src, dst) in enumerate(
            [(expo_in, expo), (rhs_in, rhs), (frac_in, frac), (comp_in, comp), (smap_in, smap)]
        )
    ]
    for copy in small:
        copy.start()

    barrier = pltpu.get_barrier_semaphore()
    for to in [sibling, *(peer(d) for d in everyone)]:
        pl.semaphore_signal(barrier, inc=1, device_id=to, device_id_type=MESH)

    for copy in small:
        copy.wait()

    picked = as_column(smap[...].astype(F32)) == iota((32, 32), 1).astype(F32)
    first = jnp.dot(
        jnp.where(picked, 1.0, 0.0).astype(BF16), rhs[...], preferred_element_type=F32
    )
    first = jnp.concatenate([first, first], axis=1).astype(BF16)
    start[0] = first[:HALF]
    start[1] = first[HALF:]
    member = iota((64, KEEP), 0) == frac[...]
    local_diag = jnp.sum(
        jnp.where(member, as_column(comp[...]), 0.0), axis=0, keepdims=True
    )
    diag_mine[...] = jnp.broadcast_to(
        jnp.concatenate([local_diag, local_diag], axis=1), (8, ROWS)
    )
    scale_row = jnp.exp2(expo[...].astype(F32)).astype(BF16).astype(F32)
    spread = jnp.where(
        (iota((CHIPS, 256), 1) >> 1) == iota((CHIPS, 256), 0), scale_row, 0.0
    ).astype(BF16)
    sides = jnp.where(
        (iota((256, ROWS), 0) & 1) == (iota((256, ROWS), 1) >> 6), 1.0, 0.0
    ).astype(BF16)
    gains[...] = jnp.dot(spread, sides, preferred_element_type=F32)

    load.wait()

    def scale(b, _):
        gain = jnp.broadcast_to(gains[pl.ds(b, 1), :], (16, ROWS)).astype(BF16)
        columns = pl.ds(pl.multiple_of(b * ROWS, ROWS), ROWS)
        for i in range(KEEP // 16):
            rows = pl.ds(pl.multiple_of(core * KEEP + 16 * i, 16), 16)
            raw[rows, columns] = raw[rows, columns] * gain
        return 0

    lax.fori_loop(0, CHIPS, scale, 0, unroll=4)

    pl.semaphore_wait(barrier, CHIPS)

    def swap(src, dst, i):
        return pltpu.make_async_remote_copy(
            src, dst, swap_send.at[i], swap_recv.at[i], device_id=sibling, device_id_type=MESH
        )

    swap_start = swap(start.at[other], started, 0)
    swap_start.start()
    swap_diag = swap(diag_mine, diag_other, 1)
    swap_diag.start()

    ours = (iota((1, ROWS), 1) >> 6) == core

    def blocks(sem, slot, count):
        part = vbuf.at[slot, pl.ds(0, count)]
        return pltpu.make_async_copy(part, part, sem)

    def send_to(slot, at, there, count, delta, sem):
        pltpu.make_async_remote_copy(
            vbuf.at[slot, pl.ds(at, count)], vbuf.at[slot, pl.ds(there, count)],
            send.at[slot], sem, device_id=peer(delta), device_id_type=MESH,
        ).start()

    def post(slot):
        for dz in ABOVE:
            place = PLACE[NZ - dz]
            group = [lo <= place < hi for lo, hi in GROUPS].index(True)
            send_to(slot, base, base + place, 1, (0, 0, dz), relay.at[slot, group])
        for delta in DIRECT:
            place = PLACE[(NZ - delta[2]) % NZ]
            send_to(slot, base, base + place, 1, delta, recv.at[slot])

    def pass_on(slot):
        for i, (lo, hi) in enumerate(GROUPS):
            blocks(relay.at[slot, i], slot, hi - max(lo, 1)).wait()
            for delta in PLANE:
                send_to(slot, base + lo, base + lo, hi - lo, delta, recv.at[slot])

    def sent(slot):
        return blocks(send.at[slot], slot, len(ABOVE) + DUE)

    swap_start.wait()
    vbuf[0, base] = jnp.where(ours, start[core], started[...])
    post(0)

    swap_rows = swap(raw.at[own_rows], raw.at[own_rows], 2)
    swap_rows.start()
    pass_on(0)
    swap_diag.wait()
    diag = jnp.where(ours, diag_mine[0:1], diag_other[0:1])
    swap_rows.wait()

    eye_rows = jnp.where(iota((ROWS, ROWS), 0) == iota((ROWS, ROWS), 1), 1.0, 0.0).astype(BF16)

    def turn(column, _):
        for place, dz in enumerate(ORDER):
            source = column * NZ + lax.rem(z + dz, NZ)
            rows = pl.ds(pl.multiple_of((column * NZ + place) * ROWS, ROWS), ROWS)
            amat[rows, :] = lax.dot_general(
                eye_rows, raw[:, pl.ds(pl.multiple_of(source * ROWS, ROWS), ROWS)],
                (((1,), (1,)), ((), ())), preferred_element_type=F32,
            ).astype(BF16)
        return 0

    lax.fori_loop(0, NX * NY, turn, 0)

    lane = iota((HALF, ROWS), 1)

    def product(step, par):
        blocks(recv.at[par], par, DUE).wait()
        sums = [jnp.zeros((HALF, ROWS), F32) for _ in range(4)]
        for b in range(CHIPS):
            value = vbuf[par, b].astype(F32)
            sums[b % 4] += value * value
        squares = jnp.sum((sums[0] + sums[1]) + (sums[2] + sums[3]), axis=1, keepdims=True)
        root = jnp.sqrt(squares / ALL + 1e-06)
        opening = step == 0
        history[core] = jnp.where(lane == step - 1, root, history[core])
        root = jnp.where(opening, 1.0, root)
        shrink = jnp.exp2(-jnp.floor(jnp.log2(root))).astype(BF16).astype(F32)
        inverse = 1.0 / root
        spread16 = jnp.broadcast_to(shrink, (HALF, ROWS)).astype(BF16)
        total = jnp.zeros((HALF, ROWS), F32)
        group = 16
        for g in range(CHIPS // group):
            part = jnp.concatenate(
                [vbuf[par, g * group + i] * spread16 for i in range(group)], axis=1
            )
            total += lax.dot_general(
                part, amat[g * group * ROWS : (g + 1) * group * ROWS, :],
                (((1,), (0,)), ((), ())), preferred_element_type=F32,
            )
        own = vbuf[par, base].astype(F32)
        return total * (inverse / shrink) + diag * (own * inverse)

    history[core] = jnp.zeros((HALF, ROWS), F32)

    def advance(step, _):
        par, nxt = lax.rem(step, SLOTS), lax.rem(step + 1, SLOTS)
        image = product(step, par)

        @pl.when(step >= 1)
        def _():
            sent(lax.rem(step + SLOTS - 1, SLOTS)).wait()

        vbuf[nxt, base] = image.astype(BF16)
        post(nxt)
        pass_on(nxt)
        return 0

    lax.fori_loop(0, STEPS - 1, advance, 0)
    image = product(STEPS - 1, (STEPS - 1) % SLOTS)

    eye = iota((HALF, ROWS), 0) == lane
    square = jnp.sum(image * image, axis=1, keepdims=True)
    norms[pl.ds(mine, 1), :] = jnp.sum(jnp.where(eye, square, 0.0), axis=0, keepdims=True)
    row = norms.at[pl.ds(mine, 1)]
    for delta in everyone:
        pltpu.make_async_remote_copy(
            row, row, norm_sem.at[0], norm_sem.at[1], device_id=peer(delta), device_id_type=MESH
        ).start()
    rows = norms.at[pl.ds(0, CHIPS - 1)]
    pltpu.make_async_copy(rows, rows, norm_sem.at[1]).wait()
    total = jnp.sum(norms[...], axis=0, keepdims=True)
    squares = jnp.sum(jnp.where(eye, total, 0.0), axis=1, keepdims=True)
    root = jnp.sqrt(squares / ALL + 1e-06)
    history[core] = jnp.where(lane == STEPS - 1, root, history[core])
    last[core] = (image / root).astype(BF16)
    swap_last = swap(last.at[core], last.at[core], 3)
    swap_history = swap(history.at[core], history.at[core], 4)
    swap_last.start()
    swap_history.start()
    pltpu.make_async_copy(rows, rows, norm_sem.at[0]).wait()
    sent((STEPS - 2) % SLOTS).wait()
    sent((STEPS - 1) % SLOTS).wait()
    swap_last.wait()
    swap_history.wait()
    result = jnp.concatenate([last[0], last[1]], axis=0).astype(F32)
    basis_out[...] = jnp.where(core == 0, result[:, :KEEP], result[:, KEEP:]).astype(BF16)
    table = jnp.concatenate([history[0], history[1]], axis=0)
    rms_out[...] = table.T[:STEPS]


def on_device(tiles, exponents, rhs, elem_frac, compliance, scen_map):
    vmem = pl.BlockSpec(memory_space=pltpu.VMEM)
    return tuple(
        pl.pallas_call(
            kernel,
            out_shape=(
                jax.ShapeDtypeStruct((32, KEEP), BF16),
                jax.ShapeDtypeStruct((STEPS, 32), F32),
            ),
            in_specs=[pl.BlockSpec(memory_space=pltpu.HBM)] * 6,
            out_specs=(vmem, vmem),
            scratch_shapes=[
                pltpu.VMEM((1, 256), jnp.int32),
                pltpu.VMEM((32, KEEP), BF16),
                pltpu.VMEM((1, KEEP), jnp.int32),
                pltpu.VMEM((1, 64), F32),
                pltpu.VMEM((1, 32), jnp.int32),
                pltpu.VMEM((ROWS, ALL), BF16),
                pltpu.VMEM((ALL, ROWS), BF16),
                pltpu.VMEM((SLOTS, CHIPS, HALF, ROWS), BF16),
                pltpu.VMEM((2, HALF, ROWS), BF16),
                pltpu.VMEM((HALF, ROWS), BF16),
                pltpu.VMEM((8, ROWS), F32),
                pltpu.VMEM((8, ROWS), F32),
                pltpu.VMEM((CHIPS, ROWS), F32),
                pltpu.VMEM((CHIPS, ROWS), F32),
                pltpu.VMEM((2, HALF, ROWS), F32),
                pltpu.VMEM((2, HALF, ROWS), BF16),
                pltpu.SemaphoreType.DMA((6,)),
                pltpu.SemaphoreType.DMA((5,)),
                pltpu.SemaphoreType.DMA((5,)),
                pltpu.SemaphoreType.DMA((SLOTS,)),
                pltpu.SemaphoreType.DMA((SLOTS,)),
                pltpu.SemaphoreType.DMA((SLOTS, NZ - 1)),
                pltpu.SemaphoreType.DMA((2,)),
            ],
            compiler_params=pltpu.CompilerParams(
                collective_id=0, has_side_effects=True, vmem_limit_bytes=63 << 20
            ),
            cost_estimate=pl.CostEstimate(
                flops=2 * STEPS * 32 * KEEP * ALL, bytes_accessed=2 * KEEP * ALL, transcendentals=0
            ),
            name="krylov",
        )(
            tiles,
            exponents,
            rhs,
            elem_frac.reshape(1, KEEP),
            compliance.reshape(1, 64),
            scen_map.reshape(1, 32),
        )
    )


def solution(mesh):
    placed = (
        P(("blk", "grp"), None),
        P(("blk", "grp"), None),
        P(None, ("blk", "grp")),
        P(("blk", "grp")),
        P(),
        P(),
    )
    return jax.shard_map(
        on_device,
        mesh=mesh,
        in_specs=placed,
        out_specs=(P(None, ("blk", "grp")), P()),
        check_vma=False,
    )
```

```python
import functools

import jax
import jax.numpy as jnp
from jax import lax
from jax.experimental import pallas as pl
from jax.experimental.pallas import tpu as pltpu
from jax.sharding import PartitionSpec as P

STEPS = 12
NX, NY, NZ = 4, 4, 8
CHIPS = NX * NY * NZ
HALF = 16
ROWS = 128
KEEP = 64
ALL = CHIPS * ROWS
MESH = pl.DeviceIdType.MESH
F32, BF16 = jnp.float32, jnp.bfloat16


def hops(delta):
    return sum(min(d, n - d) for d, n in zip(delta, (NX, NY, NZ)))


ORDER = (0, 1, 7, 2, 6, 3, 5, 4)
PLACE = {dz: i for i, dz in enumerate(ORDER)}
GROUPS = ((1, 2), (2, 3), (3, 7), (7, 8))
FAR = 6
PLANE = sorted(
    [(dx, dy, 0) for dx in range(NX) for dy in range(NY) if dx or dy], key=lambda d: -hops(d)
)
ABOVE = [(0, 0, dz) for dz in (4, 3, 5, 2, 6, 1, 7)]
DUE = CHIPS - NZ


def direct(far):
    return sorted(
        [
            (dx, dy, dz)
            for dz in range(NZ)
            for dx, dy, _ in PLANE
            if not dz or hops((dx, dy, dz)) >= far
        ],
        key=lambda d: -hops(d),
    )


NEVER = 9
SLOTS = 3


def device(blk, grp):
    return {"blk": blk, "grp": grp}


def iota(shape, dim):
    return lax.broadcasted_iota(jnp.int32, shape, dim)


def as_column(row):
    n = row.shape[1]
    eye = iota((n, n), 0) == iota((n, n), 1)
    return jnp.sum(jnp.where(eye, jnp.broadcast_to(row, (n, n)), 0.0), axis=1, keepdims=True)


def kernel(
    tiles, expo_in, rhs_in, frac_in, comp_in, smap_in, basis_out, rms_out,
    expo, rhs, frac, comp, smap, raw, amat, vbuf, start, started, diag_mine, diag_other, gains, norms, plane, history, last,
    load_sem, swap_send, swap_recv, send, recv, relay, norm_send, norm_recv,
):
    blk, grp = lax.axis_index("blk"), lax.axis_index("grp")
    x, y = lax.rem(blk, NX), lax.div(blk, NX) * 2 + lax.div(grp, 16)
    z, core = lax.rem(lax.div(grp, 2), NZ), lax.rem(grp, 2)
    other = 1 - core
    sibling = device(blk, grp + 1 - 2 * core)
    xs = [lax.rem(x + d, NX) for d in range(NX)]
    ys = [lax.rem(y + d, NY) for d in range(NY)]
    blks = [[lax.div(ys[dy], 2) * NX + xs[dx] for dy in range(NY)] for dx in range(NX)]
    low = [lax.rem(y, 2) * 16 + core, (1 - lax.rem(y, 2)) * 16 + core]
    grps = [[low[d] + 2 * lax.rem(z + dz, NZ) for dz in range(NZ)] for d in range(2)]

    def peer(delta):
        dx, dy, dz = delta
        return device(blks[dx][dy], grps[dy % 2][dz])

    known = ABOVE + PLANE
    column = lax.div(y, 2) * 8 + x * 2 + lax.rem(y, 2)
    base = column * NZ

    own_rows = pl.ds(pl.multiple_of(core * KEEP, KEEP), KEEP)
    load = pltpu.make_async_copy(tiles, raw.at[own_rows], load_sem.at[0])
    load.start()
    small = [
        pltpu.make_async_copy(src, dst, load_sem.at[1 + i])
        for i, (src, dst) in enumerate(
            [(expo_in, expo), (rhs_in, rhs), (frac_in, frac), (comp_in, comp), (smap_in, smap)]
        )
    ]
    for copy in small:
        copy.start()

    barrier = pltpu.get_barrier_semaphore()
    for to in [sibling, *(peer(d) for d in known)]:
        pl.semaphore_signal(barrier, inc=1, device_id=to, device_id_type=MESH)

    for copy in small:
        copy.wait()

    picked = as_column(smap[...].astype(F32)) == iota((32, 32), 1).astype(F32)
    first = jnp.dot(
        jnp.where(picked, 1.0, 0.0).astype(BF16), rhs[...], preferred_element_type=F32
    )
    first = jnp.concatenate([first, first], axis=1).astype(BF16)
    start[0] = first[:HALF]
    start[1] = first[HALF:]
    pl.semaphore_wait(barrier, 1 + len(known))

    def swap(src, dst, i):
        return pltpu.make_async_remote_copy(
            src, dst, swap_send.at[i], swap_recv.at[i], device_id=sibling, device_id_type=MESH
        )

    swap_start = swap(start.at[other], started, 0)
    swap_start.start()
    member = iota((64, KEEP), 0) == frac[...]
    local_diag = jnp.sum(
        jnp.where(member, as_column(comp[...]), 0.0), axis=0, keepdims=True
    )
    diag_mine[...] = jnp.broadcast_to(
        jnp.concatenate([local_diag, local_diag], axis=1), (8, ROWS)
    )
    swap_diag = swap(diag_mine, diag_other, 1)
    swap_diag.start()

    ours = (iota((1, ROWS), 1) >> 6) == core

    def blocks(sem, slot, count):
        part = vbuf.at[slot, pl.ds(0, count)]
        return pltpu.make_async_copy(part, part, sem)

    def send_to(slot, at, there, count, delta, sem):
        pltpu.make_async_remote_copy(
            vbuf.at[slot, pl.ds(at, count)], vbuf.at[slot, pl.ds(there, count)],
            send.at[slot], sem, device_id=peer(delta), device_id_type=MESH,
        ).start()

    def post(slot, far=FAR):
        for delta in ABOVE:
            place = PLACE[NZ - delta[2]]
            group = [lo <= place < hi for lo, hi in GROUPS].index(True)
            send_to(slot, base, base + place, 1, delta, relay.at[slot, group])
        for delta in direct(far):
            place = PLACE[(NZ - delta[2]) % NZ]
            send_to(slot, base, base + place, 1, delta, recv.at[slot])

    def pass_on(slot, far=FAR):
        for i, (lo, hi) in enumerate(GROUPS):
            blocks(relay.at[slot, i], slot, hi - lo).wait()
            for delta in PLANE:
                count = sum(hops((*delta[:2], ORDER[p])) < far for p in range(lo, hi))
                if count:
                    send_to(slot, base + lo, base + lo, count, delta, recv.at[slot])

    def sent(slot):
        return blocks(send.at[slot], slot, CHIPS - 1)

    swap_start.wait()
    vbuf[0, base] = jnp.where(ours, start[core], started[...])
    post(0, NEVER)

    scale_row = jnp.exp2(expo[...].astype(F32)).astype(BF16).astype(F32)
    spread = jnp.where(
        (iota((CHIPS, 256), 1) >> 1) == iota((CHIPS, 256), 0), scale_row, 0.0
    ).astype(BF16)
    sides = jnp.where(
        (iota((256, ROWS), 0) & 1) == (iota((256, ROWS), 1) >> 6), 1.0, 0.0
    ).astype(BF16)
    gains[...] = jnp.dot(spread, sides, preferred_element_type=F32)

    load.wait()

    def scale(b, _):
        gain = jnp.broadcast_to(gains[pl.ds(b, 1), :], (16, ROWS)).astype(BF16)
        columns = pl.ds(pl.multiple_of(b * ROWS, ROWS), ROWS)
        for i in range(KEEP // 16):
            rows = pl.ds(pl.multiple_of(core * KEEP + 16 * i, 16), 16)
            raw[rows, columns] = raw[rows, columns] * gain
        return 0

    lax.fori_loop(0, CHIPS, scale, 0, unroll=4)

    swap_rows = swap(raw.at[own_rows], raw.at[own_rows], 2)
    swap_rows.start()
    pass_on(0, NEVER)
    swap_diag.wait()
    diag = jnp.where(ours, diag_mine[0:1], diag_other[0:1])
    swap_rows.wait()

    lane = iota((HALF, ROWS), 1)

    def product(step, par):
        blocks(recv.at[par], par, DUE).wait()
        sums = [jnp.zeros((HALF, ROWS), F32) for _ in range(4)]
        for b in range(CHIPS):
            value = vbuf[par, b].astype(F32)
            sums[b % 4] += value * value
        squares = jnp.sum((sums[0] + sums[1]) + (sums[2] + sums[3]), axis=1, keepdims=True)
        root = jnp.sqrt(squares / ALL + 1e-06)
        history[core] = jnp.where(lane == step - 1, root, history[core])
        shrink = jnp.exp2(-jnp.floor(jnp.log2(root))).astype(BF16).astype(F32)
        inverse = 1.0 / root
        spread16 = jnp.broadcast_to(shrink, (HALF, ROWS)).astype(BF16)
        total = jnp.zeros((HALF, ROWS), F32)
        group = 16
        for g in range(CHIPS // group):
            part = jnp.concatenate(
                [vbuf[par, g * group + i] * spread16 for i in range(group)], axis=1
            )
            total += lax.dot_general(
                part, amat[g * group * ROWS : (g + 1) * group * ROWS, :],
                (((1,), (0,)), ((), ())), preferred_element_type=F32,
            )
        own = vbuf[par, base].astype(F32)
        return total * (inverse / shrink) + diag * (own * inverse)

    history[core] = jnp.zeros((HALF, ROWS), F32)

    blocks(recv.at[0], 0, DUE).wait()

    def column_product(column, total):
        parts, rows = [], []
        for place, dz in enumerate(ORDER):
            source = column * NZ + lax.rem(z + dz, NZ)
            parts.append(vbuf[0, column * NZ + place])
            rows.append(raw[:, pl.ds(pl.multiple_of(source * ROWS, ROWS), ROWS)])
        return total + lax.dot_general(
            jnp.concatenate(parts, axis=1), jnp.concatenate(rows, axis=1),
            (((1,), (1,)), ((), ())), preferred_element_type=F32,
        )

    total = lax.fori_loop(
        0, NX * NY, column_product, jnp.zeros((HALF, ROWS), F32), unroll=4
    )
    image = total + diag * vbuf[0, base].astype(F32)
    vbuf[1, base] = image.astype(BF16)
    post(1)
    pass_on(1)

    eye_rows = jnp.where(iota((ROWS, ROWS), 0) == iota((ROWS, ROWS), 1), 1.0, 0.0).astype(BF16)

    def turn(column, _):
        for place, dz in enumerate(ORDER):
            source = column * NZ + lax.rem(z + dz, NZ)
            rows = pl.ds(pl.multiple_of((column * NZ + place) * ROWS, ROWS), ROWS)
            amat[rows, :] = lax.dot_general(
                eye_rows, raw[:, pl.ds(pl.multiple_of(source * ROWS, ROWS), ROWS)],
                (((1,), (1,)), ((), ())), preferred_element_type=F32,
            ).astype(BF16)
        return 0

    lax.fori_loop(0, NX * NY, turn, 0)

    def advance(step, _):
        par, nxt = lax.rem(step, SLOTS), lax.rem(step + 1, SLOTS)
        image = product(step, par)
        sent(lax.rem(step + SLOTS - 1, SLOTS)).wait()

        vbuf[nxt, base] = image.astype(BF16)
        post(nxt)
        pass_on(nxt)
        return 0

    lax.fori_loop(1, STEPS - 1, advance, 0)
    image = product(STEPS - 1, (STEPS - 1) % SLOTS)

    def sums_of(ref, at, deltas, i):
        row = ref.at[pl.ds(at, 1)]
        for delta in deltas:
            pltpu.make_async_remote_copy(
                row, row, norm_send.at[i], norm_recv.at[i],
                device_id=peer(delta), device_id_type=MESH,
            ).start()
        rows = ref.at[pl.ds(0, len(deltas))]
        pltpu.make_async_copy(rows, rows, norm_recv.at[i]).wait()

    eye = iota((HALF, ROWS), 0) == lane
    square = jnp.sum(image * image, axis=1, keepdims=True)
    norms[pl.ds(z, 1), :] = jnp.sum(jnp.where(eye, square, 0.0), axis=0, keepdims=True)
    sums_of(norms, z, ABOVE, 0)
    plane[pl.ds(column, 1), :] = jnp.sum(norms[...], axis=0, keepdims=True)
    sums_of(plane, column, PLANE, 1)
    total = jnp.sum(plane[...], axis=0, keepdims=True)
    squares = jnp.sum(jnp.where(eye, total, 0.0), axis=1, keepdims=True)
    root = jnp.sqrt(squares / ALL + 1e-06)
    history[core] = jnp.where(lane == STEPS - 1, root, history[core])
    last[core] = (image / root).astype(BF16)
    swap_last = swap(last.at[core], last.at[core], 3)
    swap_history = swap(history.at[core], history.at[core], 4)
    swap_last.start()
    swap_history.start()
    for ref, i in ((norms, 0), (plane, 1)):
        rows = ref.at[pl.ds(0, ref.shape[0] - 1)]
        pltpu.make_async_copy(rows, rows, norm_send.at[i]).wait()
    sent((STEPS - 2) % SLOTS).wait()
    sent((STEPS - 1) % SLOTS).wait()
    swap_last.wait()
    swap_history.wait()
    result = jnp.concatenate([last[0], last[1]], axis=0).astype(F32)
    basis_out[...] = jnp.where(core == 0, result[:, :KEEP], result[:, KEEP:]).astype(BF16)
    table = jnp.concatenate([history[0], history[1]], axis=0)
    rms_out[...] = table.T[:STEPS]


def on_device(tiles, exponents, rhs, elem_frac, compliance, scen_map):
    vmem = pl.BlockSpec(memory_space=pltpu.VMEM)
    return tuple(
        pl.pallas_call(
            kernel,
            out_shape=(
                jax.ShapeDtypeStruct((32, KEEP), BF16),
                jax.ShapeDtypeStruct((STEPS, 32), F32),
            ),
            in_specs=[pl.BlockSpec(memory_space=pltpu.HBM)] * 6,
            out_specs=(vmem, vmem),
            scratch_shapes=[
                pltpu.VMEM((1, 256), jnp.int32),
                pltpu.VMEM((32, KEEP), BF16),
                pltpu.VMEM((1, KEEP), jnp.int32),
                pltpu.VMEM((1, 64), F32),
                pltpu.VMEM((1, 32), jnp.int32),
                pltpu.VMEM((ROWS, ALL), BF16),
                pltpu.VMEM((ALL, ROWS), BF16),
                pltpu.VMEM((SLOTS, CHIPS, HALF, ROWS), BF16),
                pltpu.VMEM((2, HALF, ROWS), BF16),
                pltpu.VMEM((HALF, ROWS), BF16),
                pltpu.VMEM((8, ROWS), F32),
                pltpu.VMEM((8, ROWS), F32),
                pltpu.VMEM((CHIPS, ROWS), F32),
                pltpu.VMEM((NZ, ROWS), F32),
                pltpu.VMEM((NX * NY, ROWS), F32),
                pltpu.VMEM((2, HALF, ROWS), F32),
                pltpu.VMEM((2, HALF, ROWS), BF16),
                pltpu.SemaphoreType.DMA((6,)),
                pltpu.SemaphoreType.DMA((5,)),
                pltpu.SemaphoreType.DMA((5,)),
                pltpu.SemaphoreType.DMA((SLOTS,)),
                pltpu.SemaphoreType.DMA((SLOTS,)),
                pltpu.SemaphoreType.DMA((SLOTS, NZ - 1)),
                pltpu.SemaphoreType.DMA((2,)),
                pltpu.SemaphoreType.DMA((2,)),
            ],
            compiler_params=pltpu.CompilerParams(
                collective_id=0, has_side_effects=True, vmem_limit_bytes=63 << 20
            ),
            cost_estimate=pl.CostEstimate(
                flops=2 * STEPS * 32 * KEEP * ALL, bytes_accessed=2 * KEEP * ALL, transcendentals=0
            ),
            name="krylov",
        )(
            tiles,
            exponents,
            rhs,
            elem_frac.reshape(1, KEEP),
            compliance.reshape(1, 64),
            scen_map.reshape(1, 32),
        )
    )


def solution(mesh):
    placed = (
        P(("blk", "grp"), None),
        P(("blk", "grp"), None),
        P(None, ("blk", "grp")),
        P(("blk", "grp")),
        P(),
        P(),
    )
    return jax.shard_map(
        on_device,
        mesh=mesh,
        in_specs=placed,
        out_specs=(P(None, ("blk", "grp")), P()),
        check_vma=False,
    )
```

```python
import functools

import jax
import jax.numpy as jnp
from jax import lax
from jax.experimental import pallas as pl
from jax.experimental.pallas import tpu as pltpu
from jax.sharding import PartitionSpec as P

STEPS = 12
NX, NY, NZ = 4, 4, 8
CHIPS = NX * NY * NZ
HALF = 16
ROWS = 128
KEEP = 64
ALL = CHIPS * ROWS
MESH = pl.DeviceIdType.MESH
F32, BF16 = jnp.float32, jnp.bfloat16


def hops(delta):
    return sum(min(d, n - d) for d, n in zip(delta, (NX, NY, NZ)))


ORDER = (0, 1, 7, 2, 6, 3, 5, 4)
PLACE = {dz: i for i, dz in enumerate(ORDER)}
GROUPS = ((1, 2), (2, 3), (3, 5), (5, 7), (7, 8))
FAR = 6
PLANE = sorted(
    [(dx, dy, 0) for dx in range(NX) for dy in range(NY) if dx or dy], key=lambda d: -hops(d)
)
ABOVE = [(0, 0, dz) for dz in (4, 3, 5, 2, 6, 1, 7)]
EVERYONE = sorted(
    [(dx, dy, dz) for dz in range(NZ) for dx in range(NX) for dy in range(NY) if dx or dy or dz],
    key=lambda d: -hops(d),
)
DUE = CHIPS - NZ


def direct(far):
    return sorted(
        [
            (dx, dy, dz)
            for dz in range(NZ)
            for dx, dy, _ in PLANE
            if not dz or hops((dx, dy, dz)) >= far
        ],
        key=lambda d: (-hops(d), -min(d[2], NZ - d[2]), d),
    )


NEVER = 9
SLOTS = 3


def device(blk, grp):
    return {"blk": blk, "grp": grp}


def iota(shape, dim):
    return lax.broadcasted_iota(jnp.int32, shape, dim)


def as_column(row):
    n = row.shape[1]
    eye = iota((n, n), 0) == iota((n, n), 1)
    return jnp.sum(jnp.where(eye, jnp.broadcast_to(row, (n, n)), 0.0), axis=1, keepdims=True)


def kernel(
    tiles, expo_in, rhs_in, frac_in, comp_in, smap_in, basis_out, rms_out,
    expo, rhs, frac, comp, smap, raw, amat, vbuf, start, started, diag_mine, diag_other, gains, norms, history, last,
    load_sem, swap_send, swap_recv, send, recv, relay, norm_send, norm_recv,
):
    blk, grp = lax.axis_index("blk"), lax.axis_index("grp")
    x, y = lax.rem(blk, NX), lax.div(blk, NX) * 2 + lax.div(grp, 16)
    z, core = lax.rem(lax.div(grp, 2), NZ), lax.rem(grp, 2)
    other = 1 - core
    sibling = device(blk, grp + 1 - 2 * core)
    xs = [lax.rem(x + d, NX) for d in range(NX)]
    ys = [lax.rem(y + d, NY) for d in range(NY)]
    blks = [[lax.div(ys[dy], 2) * NX + xs[dx] for dy in range(NY)] for dx in range(NX)]
    low = [lax.rem(y, 2) * 16 + core, (1 - lax.rem(y, 2)) * 16 + core]
    grps = [[low[d] + 2 * lax.rem(z + dz, NZ) for dz in range(NZ)] for d in range(2)]

    def peer(delta):
        dx, dy, dz = delta
        return device(blks[dx][dy], grps[dy % 2][dz])

    known = ABOVE + PLANE
    column = lax.div(y, 2) * 8 + x * 2 + lax.rem(y, 2)
    base = column * NZ

    own_rows = pl.ds(pl.multiple_of(core * KEEP, KEEP), KEEP)
    load = pltpu.make_async_copy(tiles, raw.at[own_rows], load_sem.at[0])
    load.start()
    small = [
        pltpu.make_async_copy(src, dst, load_sem.at[1 + i])
        for i, (src, dst) in enumerate(
            [(expo_in, expo), (rhs_in, rhs), (frac_in, frac), (comp_in, comp), (smap_in, smap)]
        )
    ]
    for copy in small:
        copy.start()

    barrier = pltpu.get_barrier_semaphore()
    for to in [sibling, *(peer(d) for d in known)]:
        pl.semaphore_signal(barrier, inc=1, device_id=to, device_id_type=MESH)

    for copy in small:
        copy.wait()

    picked = as_column(smap[...].astype(F32)) == iota((32, 32), 1).astype(F32)
    first = jnp.dot(
        jnp.where(picked, 1.0, 0.0).astype(BF16), rhs[...], preferred_element_type=F32
    )
    first = jnp.concatenate([first, first], axis=1).astype(BF16)
    start[0] = first[:HALF]
    start[1] = first[HALF:]
    pl.semaphore_wait(barrier, 1 + len(known))

    def swap(src, dst, i):
        return pltpu.make_async_remote_copy(
            src, dst, swap_send.at[i], swap_recv.at[i], device_id=sibling, device_id_type=MESH
        )

    swap_start = swap(start.at[other], started, 0)
    swap_start.start()
    member = iota((64, KEEP), 0) == frac[...]
    local_diag = jnp.sum(
        jnp.where(member, as_column(comp[...]), 0.0), axis=0, keepdims=True
    )
    diag_mine[...] = jnp.broadcast_to(
        jnp.concatenate([local_diag, local_diag], axis=1), (8, ROWS)
    )
    swap_diag = swap(diag_mine, diag_other, 1)
    swap_diag.start()

    ours = (iota((1, ROWS), 1) >> 6) == core

    def blocks(sem, slot, count):
        part = vbuf.at[slot, pl.ds(0, count)]
        return pltpu.make_async_copy(part, part, sem)

    def send_to(slot, at, there, count, delta, sem):
        pltpu.make_async_remote_copy(
            vbuf.at[slot, pl.ds(at, count)], vbuf.at[slot, pl.ds(there, count)],
            send.at[slot], sem, device_id=peer(delta), device_id_type=MESH,
        ).start()

    def post(slot, far=FAR):
        for delta in ABOVE:
            place = PLACE[NZ - delta[2]]
            group = [lo <= place < hi for lo, hi in GROUPS].index(True)
            send_to(slot, base, base + place, 1, delta, relay.at[slot, group])
        for delta in direct(far):
            place = PLACE[(NZ - delta[2]) % NZ]
            send_to(slot, base, base + place, 1, delta, recv.at[slot])

    def pass_on(slot, far=FAR):
        for i, (lo, hi) in enumerate(GROUPS):
            blocks(relay.at[slot, i], slot, hi - lo).wait()
            for delta in PLANE:
                count = sum(hops((*delta[:2], ORDER[p])) < far for p in range(lo, hi))
                if count:
                    send_to(slot, base + lo, base + lo, count, delta, recv.at[slot])

    def sent(slot):
        return blocks(send.at[slot], slot, CHIPS - 1)

    swap_start.wait()
    vbuf[0, base] = jnp.where(ours, start[core], started[...])
    post(0, NEVER)

    scale_row = jnp.exp2(expo[...].astype(F32)).astype(BF16).astype(F32)
    spread = jnp.where(
        (iota((CHIPS, 256), 1) >> 1) == iota((CHIPS, 256), 0), scale_row, 0.0
    ).astype(BF16)
    sides = jnp.where(
        (iota((256, ROWS), 0) & 1) == (iota((256, ROWS), 1) >> 6), 1.0, 0.0
    ).astype(BF16)
    gains[...] = jnp.dot(spread, sides, preferred_element_type=F32)

    load.wait()

    def scale(b, _):
        gain = jnp.broadcast_to(gains[pl.ds(b, 1), :], (16, ROWS)).astype(BF16)
        columns = pl.ds(pl.multiple_of(b * ROWS, ROWS), ROWS)
        for i in range(KEEP // 16):
            rows = pl.ds(pl.multiple_of(core * KEEP + 16 * i, 16), 16)
            raw[rows, columns] = raw[rows, columns] * gain
        return 0

    lax.fori_loop(0, CHIPS, scale, 0, unroll=4)

    swap_rows = swap(raw.at[own_rows], raw.at[own_rows], 2)
    swap_rows.start()
    pass_on(0, NEVER)
    swap_diag.wait()
    diag = jnp.where(ours, diag_mine[0:1], diag_other[0:1])
    swap_rows.wait()

    lane = iota((HALF, ROWS), 1)

    def product(step, par):
        blocks(recv.at[par], par, DUE).wait()
        sums = [jnp.zeros((HALF, ROWS), F32) for _ in range(4)]
        for b in range(CHIPS):
            value = vbuf[par, b].astype(F32)
            sums[b % 4] += value * value
        squares = jnp.sum((sums[0] + sums[1]) + (sums[2] + sums[3]), axis=1, keepdims=True)
        root = jnp.sqrt(squares / ALL + 1e-06)
        history[core] = jnp.where(lane == step - 1, root, history[core])
        shrink = jnp.exp2(-jnp.floor(jnp.log2(root))).astype(BF16).astype(F32)
        inverse = 1.0 / root
        spread16 = jnp.broadcast_to(shrink, (HALF, ROWS)).astype(BF16)
        total = jnp.zeros((HALF, ROWS), F32)
        group = 16
        for g in range(CHIPS // group):
            part = jnp.concatenate(
                [vbuf[par, g * group + i] * spread16 for i in range(group)], axis=1
            )
            total += lax.dot_general(
                part, amat[g * group * ROWS : (g + 1) * group * ROWS, :],
                (((1,), (0,)), ((), ())), preferred_element_type=F32,
            )
        own = vbuf[par, base].astype(F32)
        return total * (inverse / shrink) + diag * (own * inverse)

    history[core] = jnp.zeros((HALF, ROWS), F32)

    blocks(recv.at[0], 0, DUE).wait()

    def column_product(column, total):
        parts, rows = [], []
        for place, dz in enumerate(ORDER):
            source = column * NZ + lax.rem(z + dz, NZ)
            parts.append(vbuf[0, column * NZ + place])
            rows.append(raw[:, pl.ds(pl.multiple_of(source * ROWS, ROWS), ROWS)])
        return total + lax.dot_general(
            jnp.concatenate(parts, axis=1), jnp.concatenate(rows, axis=1),
            (((1,), (1,)), ((), ())), preferred_element_type=F32,
        )

    total = lax.fori_loop(
        0, NX * NY, column_product, jnp.zeros((HALF, ROWS), F32), unroll=4
    )
    image = total + diag * vbuf[0, base].astype(F32)
    vbuf[1, base] = image.astype(BF16)
    post(1)
    pass_on(1)

    eye_rows = jnp.where(iota((ROWS, ROWS), 0) == iota((ROWS, ROWS), 1), 1.0, 0.0).astype(BF16)

    def turn(column, _):
        for place, dz in enumerate(ORDER):
            source = column * NZ + lax.rem(z + dz, NZ)
            rows = pl.ds(pl.multiple_of((column * NZ + place) * ROWS, ROWS), ROWS)
            amat[rows, :] = lax.dot_general(
                eye_rows, raw[:, pl.ds(pl.multiple_of(source * ROWS, ROWS), ROWS)],
                (((1,), (1,)), ((), ())), preferred_element_type=F32,
            ).astype(BF16)
        return 0

    lax.fori_loop(0, NX * NY, turn, 0)

    def advance(step, _):
        par, nxt = lax.rem(step, SLOTS), lax.rem(step + 1, SLOTS)
        image = product(step, par)
        sent(lax.rem(step + SLOTS - 1, SLOTS)).wait()

        vbuf[nxt, base] = image.astype(BF16)
        post(nxt)
        pass_on(nxt)
        return 0

    lax.fori_loop(1, STEPS - 1, advance, 0)
    image = product(STEPS - 1, (STEPS - 1) % SLOTS)

    eye = iota((HALF, ROWS), 0) == lane
    square = jnp.sum(image * image, axis=1, keepdims=True)
    norms[pl.ds(base + z, 1), :] = jnp.sum(jnp.where(eye, square, 0.0), axis=0, keepdims=True)
    row = norms.at[pl.ds(base + z, 1)]
    for delta in EVERYONE:
        pltpu.make_async_remote_copy(
            row, row, norm_send, norm_recv, device_id=peer(delta), device_id_type=MESH
        ).start()
    rows = norms.at[pl.ds(0, CHIPS - 1)]
    pltpu.make_async_copy(rows, rows, norm_recv).wait()
    total = jnp.sum(norms[...], axis=0, keepdims=True)
    squares = jnp.sum(jnp.where(eye, total, 0.0), axis=1, keepdims=True)
    root = jnp.sqrt(squares / ALL + 1e-06)
    history[core] = jnp.where(lane == STEPS - 1, root, history[core])
    last[core] = (image / root).astype(BF16)
    swap_last = swap(last.at[core], last.at[core], 3)
    swap_history = swap(history.at[core], history.at[core], 4)
    swap_last.start()
    swap_history.start()
    pltpu.make_async_copy(rows, rows, norm_send).wait()
    sent((STEPS - 2) % SLOTS).wait()
    sent((STEPS - 1) % SLOTS).wait()
    swap_last.wait()
    swap_history.wait()
    result = jnp.concatenate([last[0], last[1]], axis=0).astype(F32)
    basis_out[...] = jnp.where(core == 0, result[:, :KEEP], result[:, KEEP:]).astype(BF16)
    table = jnp.concatenate([history[0], history[1]], axis=0)
    rms_out[...] = table.T[:STEPS]


def on_device(tiles, exponents, rhs, elem_frac, compliance, scen_map):
    vmem = pl.BlockSpec(memory_space=pltpu.VMEM)
    return tuple(
        pl.pallas_call(
            kernel,
            out_shape=(
                jax.ShapeDtypeStruct((32, KEEP), BF16),
                jax.ShapeDtypeStruct((STEPS, 32), F32),
            ),
            in_specs=[pl.BlockSpec(memory_space=pltpu.HBM)] * 6,
            out_specs=(vmem, vmem),
            scratch_shapes=[
                pltpu.VMEM((1, 256), jnp.int32),
                pltpu.VMEM((32, KEEP), BF16),
                pltpu.VMEM((1, KEEP), jnp.int32),
                pltpu.VMEM((1, 64), F32),
                pltpu.VMEM((1, 32), jnp.int32),
                pltpu.VMEM((ROWS, ALL), BF16),
                pltpu.VMEM((ALL, ROWS), BF16),
                pltpu.VMEM((SLOTS, CHIPS, HALF, ROWS), BF16),
                pltpu.VMEM((2, HALF, ROWS), BF16),
                pltpu.VMEM((HALF, ROWS), BF16),
                pltpu.VMEM((8, ROWS), F32),
                pltpu.VMEM((8, ROWS), F32),
                pltpu.VMEM((CHIPS, ROWS), F32),
                pltpu.VMEM((CHIPS, ROWS), F32),
                pltpu.VMEM((2, HALF, ROWS), F32),
                pltpu.VMEM((2, HALF, ROWS), BF16),
                pltpu.SemaphoreType.DMA((6,)),
                pltpu.SemaphoreType.DMA((5,)),
                pltpu.SemaphoreType.DMA((5,)),
                pltpu.SemaphoreType.DMA((SLOTS,)),
                pltpu.SemaphoreType.DMA((SLOTS,)),
                pltpu.SemaphoreType.DMA((SLOTS, NZ - 1)),
                pltpu.SemaphoreType.DMA,
                pltpu.SemaphoreType.DMA,
            ],
            compiler_params=pltpu.CompilerParams(
                collective_id=0, has_side_effects=True, vmem_limit_bytes=63 << 20
            ),
            cost_estimate=pl.CostEstimate(
                flops=2 * STEPS * 32 * KEEP * ALL, bytes_accessed=2 * KEEP * ALL, transcendentals=0
            ),
            name="krylov",
        )(
            tiles,
            exponents,
            rhs,
            elem_frac.reshape(1, KEEP),
            compliance.reshape(1, 64),
            scen_map.reshape(1, 32),
        )
    )


def solution(mesh):
    placed = (
        P(("blk", "grp"), None),
        P(("blk", "grp"), None),
        P(None, ("blk", "grp")),
        P(("blk", "grp")),
        P(),
        P(),
    )
    return jax.shard_map(
        on_device,
        mesh=mesh,
        in_specs=placed,
        out_specs=(P(None, ("blk", "grp")), P()),
        check_vma=False,
    )
```

```python
import functools

import jax
import jax.numpy as jnp
from jax import lax
from jax.experimental import pallas as pl
from jax.experimental.pallas import tpu as pltpu
from jax.sharding import PartitionSpec as P

STEPS = 12
NX, NY, NZ = 4, 4, 8
CHIPS = NX * NY * NZ
HALF = 16
ROWS = 128
KEEP = 64
ALL = CHIPS * ROWS
MESH = pl.DeviceIdType.MESH
F32, BF16 = jnp.float32, jnp.bfloat16


def hops(delta):
    return sum(min(d, n - d) for d, n in zip(delta, (NX, NY, NZ)))


ORDER = (0, 1, 7, 2, 6, 3, 5, 4)
PLACE = {dz: i for i, dz in enumerate(ORDER)}
GROUPS = ((1, 2), (2, 3), (3, 5), (5, 7), (7, 8))
FAR = 6
PLANE = sorted(
    [(dx, dy, 0) for dx in range(NX) for dy in range(NY) if dx or dy], key=lambda d: -hops(d)
)
ABOVE = [(0, 0, dz) for dz in (4, 3, 5, 2, 6, 1, 7)]
EVERYONE = sorted(
    [(dx, dy, dz) for dz in range(NZ) for dx in range(NX) for dy in range(NY) if dx or dy or dz],
    key=lambda d: -hops(d),
)
DUE = CHIPS - NZ


def direct(far):
    return sorted(
        [
            (dx, dy, dz)
            for dz in range(NZ)
            for dx, dy, _ in PLANE
            if not dz or hops((dx, dy, dz)) >= far
        ],
        key=lambda d: (-hops(d), -min(d[2], NZ - d[2]), d),
    )


NEVER = 9
SLOTS = 3


def device(blk, grp):
    return {"blk": blk, "grp": grp}


def iota(shape, dim):
    return lax.broadcasted_iota(jnp.int32, shape, dim)


def as_column(row):
    n = row.shape[1]
    eye = iota((n, n), 0) == iota((n, n), 1)
    return jnp.sum(jnp.where(eye, jnp.broadcast_to(row, (n, n)), 0.0), axis=1, keepdims=True)


def kernel(
    tiles, expo_in, rhs_in, frac_in, comp_in, smap_in, basis_out, rms_out,
    expo, rhs, frac, comp, smap, raw, amat, vbuf, start, started, diag_mine, diag_other, gains, norms, history, last,
    load_sem, swap_send, swap_recv, send, recv, relay, norm_send, norm_recv,
):
    blk, grp = lax.axis_index("blk"), lax.axis_index("grp")
    x, y = lax.rem(blk, NX), lax.div(blk, NX) * 2 + lax.div(grp, 16)
    z, core = lax.rem(lax.div(grp, 2), NZ), lax.rem(grp, 2)
    other = 1 - core
    sibling = device(blk, grp + 1 - 2 * core)
    xs = [lax.rem(x + d, NX) for d in range(NX)]
    ys = [lax.rem(y + d, NY) for d in range(NY)]
    blks = [[lax.div(ys[dy], 2) * NX + xs[dx] for dy in range(NY)] for dx in range(NX)]
    low = [lax.rem(y, 2) * 16 + core, (1 - lax.rem(y, 2)) * 16 + core]
    grps = [[low[d] + 2 * lax.rem(z + dz, NZ) for dz in range(NZ)] for d in range(2)]

    def peer(delta):
        dx, dy, dz = delta
        return device(blks[dx][dy], grps[dy % 2][dz])

    known = ABOVE + PLANE
    column = lax.div(y, 2) * 8 + x * 2 + lax.rem(y, 2)
    base = column * NZ

    own_rows = pl.ds(pl.multiple_of(core * KEEP, KEEP), KEEP)
    load = pltpu.make_async_copy(tiles, raw.at[own_rows], load_sem.at[0])
    load.start()
    small = [
        pltpu.make_async_copy(src, dst, load_sem.at[1 + i])
        for i, (src, dst) in enumerate(
            [(expo_in, expo), (rhs_in, rhs), (frac_in, frac), (comp_in, comp), (smap_in, smap)]
        )
    ]
    for copy in small:
        copy.start()

    barrier = pltpu.get_barrier_semaphore()
    for to in [sibling, *(peer(d) for d in known)]:
        pl.semaphore_signal(barrier, inc=1, device_id=to, device_id_type=MESH)

    for copy in small:
        copy.wait()

    picked = as_column(smap[...].astype(F32)) == iota((32, 32), 1).astype(F32)
    first = jnp.dot(
        jnp.where(picked, 1.0, 0.0).astype(BF16), rhs[...], preferred_element_type=F32
    )
    first = jnp.concatenate([first, first], axis=1).astype(BF16)
    start[0] = first[:HALF]
    start[1] = first[HALF:]
    pl.semaphore_wait(barrier, 1 + len(known))

    def swap(src, dst, i):
        return pltpu.make_async_remote_copy(
            src, dst, swap_send.at[i], swap_recv.at[i], device_id=sibling, device_id_type=MESH
        )

    swap_start = swap(start.at[other], started, 0)
    swap_start.start()
    member = iota((64, KEEP), 0) == frac[...]
    local_diag = jnp.sum(
        jnp.where(member, as_column(comp[...]), 0.0), axis=0, keepdims=True
    )
    diag_mine[...] = jnp.broadcast_to(
        jnp.concatenate([local_diag, local_diag], axis=1), (8, ROWS)
    )
    swap_diag = swap(diag_mine, diag_other, 1)
    swap_diag.start()

    ours = (iota((1, ROWS), 1) >> 6) == core

    def blocks(sem, slot, count):
        part = vbuf.at[slot, pl.ds(0, count)]
        return pltpu.make_async_copy(part, part, sem)

    def send_to(slot, at, there, count, delta, sem):
        pltpu.make_async_remote_copy(
            vbuf.at[slot, pl.ds(at, count)], vbuf.at[slot, pl.ds(there, count)],
            send.at[slot], sem, device_id=peer(delta), device_id_type=MESH,
        ).start()

    def post(slot, far=FAR):
        for delta in ABOVE:
            place = PLACE[NZ - delta[2]]
            group = [lo <= place < hi for lo, hi in GROUPS].index(True)
            send_to(slot, base, base + place, 1, delta, relay.at[slot, group])
        for delta in direct(far):
            place = PLACE[(NZ - delta[2]) % NZ]
            send_to(slot, base, base + place, 1, delta, recv.at[slot])

    def pass_on(slot, far=FAR):
        for i, (lo, hi) in enumerate(GROUPS):
            blocks(relay.at[slot, i], slot, hi - lo).wait()
            for delta in PLANE:
                count = sum(hops((*delta[:2], ORDER[p])) < far for p in range(lo, hi))
                if count:
                    send_to(slot, base + lo, base + lo, count, delta, recv.at[slot])

    def sent(slot):
        return blocks(send.at[slot], slot, CHIPS - 1)

    swap_start.wait()
    vbuf[0, base] = jnp.where(ours, start[core], started[...])
    post(0, NEVER)

    scale_row = jnp.exp2(expo[...].astype(F32)).astype(BF16).astype(F32)
    spread = jnp.where(
        (iota((CHIPS, 256), 1) >> 1) == iota((CHIPS, 256), 0), scale_row, 0.0
    ).astype(BF16)
    sides = jnp.where(
        (iota((256, ROWS), 0) & 1) == (iota((256, ROWS), 1) >> 6), 1.0, 0.0
    ).astype(BF16)
    gains[...] = jnp.dot(spread, sides, preferred_element_type=F32)

    load.wait()

    def scale(b, _):
        gain = jnp.broadcast_to(gains[pl.ds(b, 1), :], (16, ROWS)).astype(BF16)
        columns = pl.ds(pl.multiple_of(b * ROWS, ROWS), ROWS)
        for i in range(KEEP // 16):
            rows = pl.ds(pl.multiple_of(core * KEEP + 16 * i, 16), 16)
            raw[rows, columns] = raw[rows, columns] * gain
        return 0

    lax.fori_loop(0, CHIPS, scale, 0, unroll=4)

    swap_rows = swap(raw.at[own_rows], raw.at[own_rows], 2)
    swap_rows.start()
    pass_on(0, NEVER)
    swap_diag.wait()
    diag = jnp.where(ours, diag_mine[0:1], diag_other[0:1])
    swap_rows.wait()

    lane = iota((HALF, ROWS), 1)

    def product(step, par):
        blocks(recv.at[par], par, DUE).wait()
        sums = [jnp.zeros((HALF, ROWS), F32) for _ in range(4)]
        for b in range(CHIPS):
            value = vbuf[par, b].astype(F32)
            sums[b % 4] += value * value
        squares = jnp.sum((sums[0] + sums[1]) + (sums[2] + sums[3]), axis=1, keepdims=True)
        root = jnp.sqrt(squares / ALL + 1e-06)
        history[core] = jnp.where(lane == step - 1, root, history[core])
        shrink = jnp.exp2(-jnp.floor(jnp.log2(root))).astype(BF16).astype(F32)
        inverse = 1.0 / root
        spread16 = jnp.broadcast_to(shrink, (HALF, ROWS)).astype(BF16)
        total = jnp.zeros((HALF, ROWS), F32)
        group = 16
        for g in range(CHIPS // group):
            part = jnp.concatenate(
                [vbuf[par, g * group + i] * spread16 for i in range(group)], axis=1
            )
            total += lax.dot_general(
                part, amat[g * group * ROWS : (g + 1) * group * ROWS, :],
                (((1,), (0,)), ((), ())), preferred_element_type=F32,
            )
        own = vbuf[par, base].astype(F32)
        return total * (inverse / shrink) + diag * (own * inverse)

    history[core] = jnp.zeros((HALF, ROWS), F32)

    blocks(recv.at[0], 0, DUE).wait()

    def column_product(column, total):
        parts, rows = [], []
        for place, dz in enumerate(ORDER):
            source = column * NZ + lax.rem(z + dz, NZ)
            parts.append(vbuf[0, column * NZ + place])
            rows.append(raw[:, pl.ds(pl.multiple_of(source * ROWS, ROWS), ROWS)])
        return total + lax.dot_general(
            jnp.concatenate(parts, axis=1), jnp.concatenate(rows, axis=1),
            (((1,), (1,)), ((), ())), preferred_element_type=F32,
        )

    total = lax.fori_loop(
        0, NX * NY, column_product, jnp.zeros((HALF, ROWS), F32), unroll=4
    )
    image = total + diag * vbuf[0, base].astype(F32)
    vbuf[1, base] = image.astype(BF16)
    post(1)
    pass_on(1)

    eye_rows = jnp.where(iota((ROWS, ROWS), 0) == iota((ROWS, ROWS), 1), 1.0, 0.0).astype(BF16)

    def turn(column, _):
        for place, dz in enumerate(ORDER):
            source = column * NZ + lax.rem(z + dz, NZ)
            rows = pl.ds(pl.multiple_of((column * NZ + place) * ROWS, ROWS), ROWS)
            amat[rows, :] = lax.dot_general(
                eye_rows, raw[:, pl.ds(pl.multiple_of(source * ROWS, ROWS), ROWS)],
                (((1,), (1,)), ((), ())), preferred_element_type=F32,
            ).astype(BF16)
        return 0

    lax.fori_loop(0, NX * NY, turn, 0)

    def advance(step, _):
        par, nxt = lax.rem(step, SLOTS), lax.rem(step + 1, SLOTS)
        image = product(step, par)
        sent(lax.rem(step + SLOTS - 1, SLOTS)).wait()

        vbuf[nxt, base] = image.astype(BF16)
        post(nxt)
        pass_on(nxt)
        return 0

    lax.fori_loop(1, STEPS - 1, advance, 0)
    image = product(STEPS - 1, (STEPS - 1) % SLOTS)

    eye = iota((HALF, ROWS), 0) == lane
    square = jnp.sum(image * image, axis=1, keepdims=True)
    norms[pl.ds(base + z, 1), :] = jnp.sum(jnp.where(eye, square, 0.0), axis=0, keepdims=True)
    row = norms.at[pl.ds(base + z, 1)]
    for delta in EVERYONE:
        pltpu.make_async_remote_copy(
            row, row, norm_send, norm_recv, device_id=peer(delta), device_id_type=MESH
        ).start()
    rows = norms.at[pl.ds(0, CHIPS - 1)]
    pltpu.make_async_copy(rows, rows, norm_recv).wait()
    total = jnp.sum(norms[...], axis=0, keepdims=True)
    squares = jnp.sum(jnp.where(eye, total, 0.0), axis=1, keepdims=True)
    root = jnp.sqrt(squares / ALL + 1e-06)
    history[core] = jnp.where(lane == STEPS - 1, root, history[core])
    last[core] = (image / root).astype(BF16)
    swap_last = swap(last.at[core], last.at[core], 3)
    swap_history = swap(history.at[core], history.at[core], 4)
    swap_last.start()
    swap_history.start()
    pltpu.make_async_copy(rows, rows, norm_send).wait()
    sent((STEPS - 2) % SLOTS).wait()
    sent((STEPS - 1) % SLOTS).wait()
    swap_last.wait()
    swap_history.wait()
    result = jnp.concatenate([last[0], last[1]], axis=0).astype(F32)
    basis_out[...] = jnp.where(core == 0, result[:, :KEEP], result[:, KEEP:]).astype(BF16)
    table = jnp.concatenate([history[0], history[1]], axis=0)
    rms_out[...] = table.T[:STEPS]


def on_device(tiles, exponents, rhs, elem_frac, compliance, scen_map):
    vmem = pl.BlockSpec(memory_space=pltpu.VMEM)
    return tuple(
        pl.pallas_call(
            kernel,
            out_shape=(
                pltpu.VMEM((32, KEEP), BF16),
                pltpu.VMEM((STEPS, 32), F32),
            ),
            in_specs=[pl.BlockSpec(memory_space=pltpu.HBM)] * 6,
            out_specs=(vmem, vmem),
            scratch_shapes=[
                pltpu.VMEM((1, 256), jnp.int32),
                pltpu.VMEM((32, KEEP), BF16),
                pltpu.VMEM((1, KEEP), jnp.int32),
                pltpu.VMEM((1, 64), F32),
                pltpu.VMEM((1, 32), jnp.int32),
                pltpu.VMEM((ROWS, ALL), BF16),
                pltpu.VMEM((ALL, ROWS), BF16),
                pltpu.VMEM((SLOTS, CHIPS, HALF, ROWS), BF16),
                pltpu.VMEM((2, HALF, ROWS), BF16),
                pltpu.VMEM((HALF, ROWS), BF16),
                pltpu.VMEM((8, ROWS), F32),
                pltpu.VMEM((8, ROWS), F32),
                pltpu.VMEM((CHIPS, ROWS), F32),
                pltpu.VMEM((CHIPS, ROWS), F32),
                pltpu.VMEM((2, HALF, ROWS), F32),
                pltpu.VMEM((2, HALF, ROWS), BF16),
                pltpu.SemaphoreType.DMA((6,)),
                pltpu.SemaphoreType.DMA((5,)),
                pltpu.SemaphoreType.DMA((5,)),
                pltpu.SemaphoreType.DMA((SLOTS,)),
                pltpu.SemaphoreType.DMA((SLOTS,)),
                pltpu.SemaphoreType.DMA((SLOTS, NZ - 1)),
                pltpu.SemaphoreType.DMA,
                pltpu.SemaphoreType.DMA,
            ],
            compiler_params=pltpu.CompilerParams(
                collective_id=0, has_side_effects=True, vmem_limit_bytes=63 << 20
            ),
            cost_estimate=pl.CostEstimate(
                flops=2 * STEPS * 32 * KEEP * ALL, bytes_accessed=2 * KEEP * ALL, transcendentals=0
            ),
            name="krylov",
        )(
            tiles,
            exponents,
            rhs,
            elem_frac.reshape(1, KEEP),
            compliance.reshape(1, 64),
            scen_map.reshape(1, 32),
        )
    )


def solution(mesh):
    placed = (
        P(("blk", "grp"), None),
        P(("blk", "grp"), None),
        P(None, ("blk", "grp")),
        P(("blk", "grp")),
        P(),
        P(),
    )
    return jax.shard_map(
        on_device,
        mesh=mesh,
        in_specs=placed,
        out_specs=(P(None, ("blk", "grp")), P()),
        check_vma=False,
    )
```

```python
import functools

import jax
import jax.numpy as jnp
from jax import lax
from jax.experimental import pallas as pl
from jax.experimental.pallas import tpu as pltpu
from jax.sharding import PartitionSpec as P

STEPS = 12
NX, NY, NZ = 4, 4, 8
CHIPS = NX * NY * NZ
HALF = 16
ROWS = 128
KEEP = 64
ALL = CHIPS * ROWS
MESH = pl.DeviceIdType.MESH
F32, BF16 = jnp.float32, jnp.bfloat16


def hops(delta):
    return sum(min(d, n - d) for d, n in zip(delta, (NX, NY, NZ)))


ORDER = (0, 1, 7, 2, 6, 3, 5, 4)
PLACE = {dz: i for i, dz in enumerate(ORDER)}
GROUPS = ((1, 2), (2, 3), (3, 5), (5, 7), (7, 8))
FAR = 6
PLANE = sorted(
    [(dx, dy, 0) for dx in range(NX) for dy in range(NY) if dx or dy], key=lambda d: -hops(d)
)
ABOVE = [(0, 0, dz) for dz in (4, 3, 5, 2, 6, 1, 7)]
EVERYONE = sorted(
    [(dx, dy, dz) for dz in range(NZ) for dx in range(NX) for dy in range(NY) if dx or dy or dz],
    key=lambda d: -hops(d),
)
DUE = CHIPS - NZ


def direct(far):
    return sorted(
        [
            (dx, dy, dz)
            for dz in range(NZ)
            for dx, dy, _ in PLANE
            if not dz or hops((dx, dy, dz)) >= far
        ],
        key=lambda d: (-hops(d), -min(d[2], NZ - d[2]), d),
    )


NEVER = 9
SLOTS = 3


def device(blk, grp):
    return {"blk": blk, "grp": grp}


def iota(shape, dim):
    return lax.broadcasted_iota(jnp.int32, shape, dim)


def as_column(row):
    n = row.shape[1]
    eye = iota((n, n), 0) == iota((n, n), 1)
    return jnp.sum(jnp.where(eye, jnp.broadcast_to(row, (n, n)), 0.0), axis=1, keepdims=True)


def kernel(
    tiles, expo_in, rhs_in, frac_in, comp_in, smap_in, basis_out, rms_out,
    expo, rhs, frac, comp, smap, raw, amat, vbuf, start, started, diag_mine, diag_other, gains, norms, history, last,
    load_sem, swap_send, swap_recv, send, recv, relay, norm_send, norm_recv,
):
    blk, grp = lax.axis_index("blk"), lax.axis_index("grp")
    x, y = lax.rem(blk, NX), lax.div(blk, NX) * 2 + lax.div(grp, 16)
    z, core = lax.rem(lax.div(grp, 2), NZ), lax.rem(grp, 2)
    other = 1 - core
    sibling = device(blk, grp + 1 - 2 * core)
    xs = [lax.rem(x + d, NX) for d in range(NX)]
    ys = [lax.rem(y + d, NY) for d in range(NY)]
    blks = [[lax.div(ys[dy], 2) * NX + xs[dx] for dy in range(NY)] for dx in range(NX)]
    low = [lax.rem(y, 2) * 16 + core, (1 - lax.rem(y, 2)) * 16 + core]
    grps = [[low[d] + 2 * lax.rem(z + dz, NZ) for dz in range(NZ)] for d in range(2)]

    def peer(delta):
        dx, dy, dz = delta
        return device(blks[dx][dy], grps[dy % 2][dz])

    known = ABOVE + PLANE
    column = lax.div(y, 2) * 8 + x * 2 + lax.rem(y, 2)
    base = column * NZ

    own_rows = pl.ds(pl.multiple_of(core * KEEP, KEEP), KEEP)
    load = pltpu.make_async_copy(tiles, raw.at[own_rows], load_sem.at[0])
    load.start()
    small = [
        pltpu.make_async_copy(src, dst, load_sem.at[1 + i])
        for i, (src, dst) in enumerate(
            [(expo_in, expo), (rhs_in, rhs), (frac_in, frac), (comp_in, comp), (smap_in, smap)]
        )
    ]
    for copy in small:
        copy.start()

    barrier = pltpu.get_barrier_semaphore()
    for to in [sibling, *(peer(d) for d in known)]:
        pl.semaphore_signal(barrier, inc=1, device_id=to, device_id_type=MESH)

    for copy in small:
        copy.wait()

    picked = as_column(smap[...].astype(F32)) == iota((32, 32), 1).astype(F32)
    first = jnp.dot(
        jnp.where(picked, 1.0, 0.0).astype(BF16), rhs[...], preferred_element_type=F32
    )
    first = jnp.concatenate([first, first], axis=1).astype(BF16)
    start[0] = first[:HALF]
    start[1] = first[HALF:]
    pl.semaphore_wait(barrier, 1 + len(known))

    def swap(src, dst, i):
        return pltpu.make_async_remote_copy(
            src, dst, swap_send.at[i], swap_recv.at[i], device_id=sibling, device_id_type=MESH
        )

    swap_start = swap(start.at[other], started, 0)
    swap_start.start()
    member = iota((64, KEEP), 0) == frac[...]
    local_diag = jnp.sum(
        jnp.where(member, as_column(comp[...]), 0.0), axis=0, keepdims=True
    )
    diag_mine[...] = jnp.broadcast_to(
        jnp.concatenate([local_diag, local_diag], axis=1), (8, ROWS)
    )
    swap_diag = swap(diag_mine, diag_other, 1)
    swap_diag.start()

    ours = (iota((1, ROWS), 1) >> 6) == core

    def blocks(sem, slot, count):
        part = vbuf.at[slot, pl.ds(0, count)]
        return pltpu.make_async_copy(part, part, sem)

    def send_to(slot, at, there, count, delta, sem):
        pltpu.make_async_remote_copy(
            vbuf.at[slot, pl.ds(at, count)], vbuf.at[slot, pl.ds(there, count)],
            send.at[slot], sem, device_id=peer(delta), device_id_type=MESH,
        ).start()

    def post(slot, far=FAR):
        for delta in ABOVE:
            place = PLACE[NZ - delta[2]]
            group = [lo <= place < hi for lo, hi in GROUPS].index(True)
            send_to(slot, base, base + place, 1, delta, relay.at[slot, group])
        for delta in direct(far):
            place = PLACE[(NZ - delta[2]) % NZ]
            send_to(slot, base, base + place, 1, delta, recv.at[slot])

    def pass_on(slot, far=FAR):
        for i, (lo, hi) in enumerate(GROUPS):
            blocks(relay.at[slot, i], slot, hi - lo).wait()
            for delta in PLANE:
                count = sum(hops((*delta[:2], ORDER[p])) < far for p in range(lo, hi))
                if count:
                    send_to(slot, base + lo, base + lo, count, delta, recv.at[slot])

    def sent(slot):
        return blocks(send.at[slot], slot, CHIPS - 1)

    swap_start.wait()
    vbuf[0, base] = jnp.where(ours, start[core], started[...])
    post(0, NEVER)

    scale_row = jnp.exp2(expo[...].astype(F32)).astype(BF16).astype(F32)
    spread = jnp.where(
        (iota((CHIPS, 256), 1) >> 1) == iota((CHIPS, 256), 0), scale_row, 0.0
    ).astype(BF16)
    sides = jnp.where(
        (iota((256, ROWS), 0) & 1) == (iota((256, ROWS), 1) >> 6), 1.0, 0.0
    ).astype(BF16)
    gains[...] = jnp.dot(spread, sides, preferred_element_type=F32)

    load.wait()

    def scale(b, _):
        gain = jnp.broadcast_to(gains[pl.ds(b, 1), :], (16, ROWS)).astype(BF16)
        columns = pl.ds(pl.multiple_of(b * ROWS, ROWS), ROWS)
        for i in range(KEEP // 16):
            rows = pl.ds(pl.multiple_of(core * KEEP + 16 * i, 16), 16)
            raw[rows, columns] = raw[rows, columns] * gain
        return 0

    lax.fori_loop(0, CHIPS, scale, 0, unroll=4)

    swap_rows = swap(raw.at[own_rows], raw.at[own_rows], 2)
    swap_rows.start()
    pass_on(0, NEVER)
    swap_diag.wait()
    diag = jnp.where(ours, diag_mine[0:1], diag_other[0:1])
    swap_rows.wait()

    lane = iota((HALF, ROWS), 1)

    def product(step, par):
        blocks(recv.at[par], par, DUE).wait()
        sums = [jnp.zeros((HALF, ROWS), F32) for _ in range(8)]
        for b in range(CHIPS):
            value = vbuf[par, b].astype(F32)
            sums[b % 8] += value * value
        squares = jnp.sum(((sums[0] + sums[1]) + (sums[2] + sums[3])) + ((sums[4] + sums[5]) + (sums[6] + sums[7])), axis=1, keepdims=True)
        mean = squares / ALL + 1e-06
        shrink = jnp.exp2(-jnp.floor(0.5 * jnp.log2(mean))).astype(BF16).astype(F32)
        root = jnp.sqrt(mean)
        inverse = 1.0 / root
        spread16 = jnp.broadcast_to(shrink, (HALF, ROWS)).astype(BF16)
        total = jnp.zeros((HALF, ROWS), F32)
        group = 16
        for g in range(CHIPS // group):
            part = jnp.concatenate(
                [vbuf[par, g * group + i] * spread16 for i in range(group)], axis=1
            )
            total += lax.dot_general(
                part, amat[g * group * ROWS : (g + 1) * group * ROWS, :],
                (((1,), (0,)), ((), ())), preferred_element_type=F32,
            )
        history[core] = jnp.where(lane == step - 1, root, history[core])
        own = vbuf[par, base].astype(F32)
        return total * (inverse / shrink) + diag * (own * inverse)

    history[core] = jnp.zeros((HALF, ROWS), F32)

    blocks(recv.at[0], 0, DUE).wait()

    def column_product(column, total):
        parts, rows = [], []
        for place, dz in enumerate(ORDER):
            source = column * NZ + lax.rem(z + dz, NZ)
            parts.append(vbuf[0, column * NZ + place])
            rows.append(raw[:, pl.ds(pl.multiple_of(source * ROWS, ROWS), ROWS)])
        return total + lax.dot_general(
            jnp.concatenate(parts, axis=1), jnp.concatenate(rows, axis=1),
            (((1,), (1,)), ((), ())), preferred_element_type=F32,
        )

    total = lax.fori_loop(
        0, NX * NY, column_product, jnp.zeros((HALF, ROWS), F32), unroll=4
    )
    image = total + diag * vbuf[0, base].astype(F32)
    vbuf[1, base] = image.astype(BF16)
    post(1)
    pass_on(1)

    eye_rows = jnp.where(iota((ROWS, ROWS), 0) == iota((ROWS, ROWS), 1), 1.0, 0.0).astype(BF16)

    def turn(column, _):
        for place, dz in enumerate(ORDER):
            source = column * NZ + lax.rem(z + dz, NZ)
            rows = pl.ds(pl.multiple_of((column * NZ + place) * ROWS, ROWS), ROWS)
            amat[rows, :] = lax.dot_general(
                eye_rows, raw[:, pl.ds(pl.multiple_of(source * ROWS, ROWS), ROWS)],
                (((1,), (1,)), ((), ())), preferred_element_type=F32,
            ).astype(BF16)
        return 0

    lax.fori_loop(0, NX * NY, turn, 0)

    def advance(step, _):
        par, nxt = lax.rem(step, SLOTS), lax.rem(step + 1, SLOTS)
        image = product(step, par)
        sent(lax.rem(step + SLOTS - 1, SLOTS)).wait()

        vbuf[nxt, base] = image.astype(BF16)
        post(nxt)
        pass_on(nxt)
        return 0

    lax.fori_loop(1, STEPS - 1, advance, 0)
    image = product(STEPS - 1, (STEPS - 1) % SLOTS)

    eye = iota((HALF, ROWS), 0) == lane
    square = jnp.sum(image * image, axis=1, keepdims=True)
    norms[pl.ds(base + z, 1), :] = jnp.sum(jnp.where(eye, square, 0.0), axis=0, keepdims=True)
    row = norms.at[pl.ds(base + z, 1)]
    for delta in EVERYONE:
        pltpu.make_async_remote_copy(
            row, row, norm_send, norm_recv, device_id=peer(delta), device_id_type=MESH
        ).start()
    rows = norms.at[pl.ds(0, CHIPS - 1)]
    pltpu.make_async_copy(rows, rows, norm_recv).wait()
    total = jnp.sum(norms[...], axis=0, keepdims=True)
    squares = jnp.sum(jnp.where(eye, total, 0.0), axis=1, keepdims=True)
    root = jnp.sqrt(squares / ALL + 1e-06)
    history[core] = jnp.where(lane == STEPS - 1, root, history[core])
    last[core] = (image / root).astype(BF16)
    swap_last = swap(last.at[core], last.at[core], 3)
    swap_history = swap(history.at[core], history.at[core], 4)
    swap_last.start()
    swap_history.start()
    pltpu.make_async_copy(rows, rows, norm_send).wait()
    sent((STEPS - 2) % SLOTS).wait()
    sent((STEPS - 1) % SLOTS).wait()
    swap_last.wait()
    swap_history.wait()
    result = jnp.concatenate([last[0], last[1]], axis=0).astype(F32)
    basis_out[...] = jnp.where(core == 0, result[:, :KEEP], result[:, KEEP:]).astype(BF16)
    table = jnp.concatenate([history[0], history[1]], axis=0)
    rms_out[...] = table.T[:STEPS]


def on_device(tiles, exponents, rhs, elem_frac, compliance, scen_map):
    vmem = pl.BlockSpec(memory_space=pltpu.VMEM)
    return tuple(
        pl.pallas_call(
            kernel,
            out_shape=(
                pltpu.VMEM((32, KEEP), BF16),
                pltpu.VMEM((STEPS, 32), F32),
            ),
            in_specs=[pl.BlockSpec(memory_space=pltpu.HBM)] * 6,
            out_specs=(vmem, vmem),
            scratch_shapes=[
                pltpu.VMEM((1, 256), jnp.int32),
                pltpu.VMEM((32, KEEP), BF16),
                pltpu.VMEM((1, KEEP), jnp.int32),
                pltpu.VMEM((1, 64), F32),
                pltpu.VMEM((1, 32), jnp.int32),
                pltpu.VMEM((ROWS, ALL), BF16),
                pltpu.VMEM((ALL, ROWS), BF16),
                pltpu.VMEM((SLOTS, CHIPS, HALF, ROWS), BF16),
                pltpu.VMEM((2, HALF, ROWS), BF16),
                pltpu.VMEM((HALF, ROWS), BF16),
                pltpu.VMEM((8, ROWS), F32),
                pltpu.VMEM((8, ROWS), F32),
                pltpu.VMEM((CHIPS, ROWS), F32),
                pltpu.VMEM((CHIPS, ROWS), F32),
                pltpu.VMEM((2, HALF, ROWS), F32),
                pltpu.VMEM((2, HALF, ROWS), BF16),
                pltpu.SemaphoreType.DMA((6,)),
                pltpu.SemaphoreType.DMA((5,)),
                pltpu.SemaphoreType.DMA((5,)),
                pltpu.SemaphoreType.DMA((SLOTS,)),
                pltpu.SemaphoreType.DMA((SLOTS,)),
                pltpu.SemaphoreType.DMA((SLOTS, NZ - 1)),
                pltpu.SemaphoreType.DMA,
                pltpu.SemaphoreType.DMA,
            ],
            compiler_params=pltpu.CompilerParams(
                collective_id=0, has_side_effects=True, vmem_limit_bytes=63 << 20
            ),
            cost_estimate=pl.CostEstimate(
                flops=2 * STEPS * 32 * KEEP * ALL, bytes_accessed=2 * KEEP * ALL, transcendentals=0
            ),
            name="krylov",
        )(
            tiles,
            exponents,
            rhs,
            elem_frac.reshape(1, KEEP),
            compliance.reshape(1, 64),
            scen_map.reshape(1, 32),
        )
    )


def solution(mesh):
    placed = (
        P(("blk", "grp"), None),
        P(("blk", "grp"), None),
        P(None, ("blk", "grp")),
        P(("blk", "grp")),
        P(),
        P(),
    )
    return jax.shard_map(
        on_device,
        mesh=mesh,
        in_specs=placed,
        out_specs=(P(None, ("blk", "grp")), P()),
        check_vma=False,
    )
```
